32 devices in a mesh: dp: 8 (over z, y), mp: 4 (over x, core).
Axes of the slice: x: 2, y: 2, z: 4, core: 2. Of those that a mesh axis runs over, the one named last changes fastest.
Arguments:
- tokens: bfloat16 [4096, 768], P(('dp', 'mp')), may hold values from -6 to 6
- teacher: bfloat16 [4096, 768], P(('dp', 'mp')), may hold values from -6 to 6
- segments: int32 [4096], P('dp'), may hold values from 0 to 31, never falling along the last dimension, each value on 1 to 512 neighbouring positions
- valid_mask: int32 [4096], P('dp'), may hold values from 0 to 1, as said below
- routes: int32 [4096, 2], P('dp'), may hold values from 0 to 15, all different within a row; in each aligned block of 512 rows (0 to 511, 512 to 1023, ...) at most 128 rows name the same one
- first_gain: float32 [768], replicated, may hold values from 0.5 to 1.5
- second_gain: float32 [768], replicated, may hold values from 0.5 to 1.5
- router_weight: float32 [768, 16], replicated, may hold values from -0.21875 to 0.21875
- attention_in: float32 [768, 3, 768], P('dp', None, 'mp'), may hold values from -0.21875 to 0.21875
- attention_out: float32 [768, 768], P('dp', 'mp'), may hold values from -1.25 to 1.25
- dense_in: float32 [768, 2, 2048], P('dp', None, 'mp'), may hold values from -0.21875 to 0.21875
- dense_out: float32 [768, 2048], P('dp', 'mp'), may hold values from -0.125 to 0.125
- expert_in: float32 [16, 768, 2, 2048], P('dp', None, None, 'mp'), may hold values from -0.21875 to 0.21875
- expert_out: float32 [16, 768, 2048], P('dp', None, 'mp'), may hold values from -0.125 to 0.125
- moment_first_gain: float32 [768], replicated, may hold values from -192 to 192
- moment_second_gain: float32 [768], replicated, may hold values from -192 to 192
- moment_router: float32 [768, 16], replicated, may hold values from -21760 to 21760
- moment_attention_in: float32 [768, 3, 768], P('dp', None, 'mp'), may hold values from -21760 to 21760
- moment_attention_out: float32 [768, 768], P('dp', 'mp'), may hold values from -80 to 80
- moment_dense_in: float32 [768, 2, 2048], P('dp', None, 'mp'), may hold values from -80 to 80
- moment_dense_out: float32 [768, 2048], P('dp', 'mp'), may hold values from -80 to 80
- moment_expert_in: float32 [16, 768, 2, 2048], P('dp', None, None, 'mp'), may hold values from -14 to 14
- moment_expert_out: float32 [16, 768, 2048], P('dp', None, 'mp'), may hold values from -14 to 14
Outputs:
- output: bfloat16 [4096, 768], P(('dp', 'mp'))
- loss_value: float32 [], replicated
- grad_tokens: float32 [4096, 768], P(('dp', 'mp'))
- grad_first_gain: float32 [768], replicated
- grad_second_gain: float32 [768], replicated
- grad_router: float32 [768, 16], replicated
- grad_attention_in: float32 [768, 3, 768], P('dp', None, 'mp')
- grad_attention_out: float32 [768, 768], P('dp', 'mp')
- grad_dense_in: float32 [768, 2, 2048], P('dp', None, 'mp')
- grad_dense_out: float32 [768, 2048], P('dp', 'mp')
- grad_expert_in: float32 [16, 768, 2, 2048], P('dp', None, None, 'mp')
- grad_expert_out: float32 [16, 768, 2048], P('dp', None, 'mp')
- new_moment_first_gain: float32 [768], replicated
- new_moment_second_gain: float32 [768], replicated
- new_moment_router: float32 [768, 16], replicated
- new_moment_attention_in: float32 [768, 3, 768], P('dp', None, 'mp')
- new_moment_attention_out: float32 [768, 768], P('dp', 'mp')
- new_moment_dense_in: float32 [768, 2, 2048], P('dp', None, 'mp')
- new_moment_dense_out: float32 [768, 2048], P('dp', 'mp')
- new_moment_expert_in: float32 [16, 768, 2, 2048], P('dp', None, None, 'mp')
- new_moment_expert_out: float32 [16, 768, 2048], P('dp', None, 'mp')
- step_first_gain: float32 [768], replicated
- step_second_gain: float32 [768], replicated
- new_router: float32 [768, 16], replicated
- new_attention_in: float32 [768, 3, 768], P('dp', None, 'mp')
- step_attention_out: float32 [768, 768], P('dp', 'mp')
- new_dense_in: float32 [768, 2, 2048], P('dp', None, 'mp')
- new_dense_out: float32 [768, 2048], P('dp', 'mp')
- new_expert_in: float32 [16, 768, 2, 2048], P('dp', None, None, 'mp')
- new_expert_out: float32 [16, 768, 2048], P('dp', None, 'mp')
The draws below stay inside these ranges and needn't reach their ends.
Inputs may be any that keep to these rules, and one draw needn't show every extreme that they name: `valid_mask`: within each sequence of 512 tokens, valid tokens come first and padding follows. `routes`: A token names two different experts; within the 512 rows of one sequence no expert is named more than 128 times.
All inputs are finite; a program needn't handle non-finite values.
Results may differ from the reference program's by a relative error of at most 0.017.
Values may be sent and summed in bfloat16 or wider, within the bound.
No kernel may reach another device: no remote copies, remote signals or barrier semaphores. Data moves between devices by JAX's collectives and lax.ppermute only.
A program may use at most 256 MiB of HBM per device.

```python
import math
import jax
import jax.numpy as jnp
import numpy as np
from jax import lax

D = 768
HEADS = 12
HEAD_DIM = 64
HQ = 768
FF = 2048
EXPERTS = 16
EQ = 1
SEQ = 512
TOKENS = 4096
CAP = 128
NS_ITERS = 2
N_MP = 4


def draw_valid_mask(key, part):
    groups = TOKENS // SEQ
    extra = jax.random.randint(key, (groups,), 0, max(SEQ // 16, 1))
    padding = jnp.arange(groups, dtype=jnp.int32) * (2 * SEQ // 3) // groups + extra
    positions = jnp.arange(TOKENS, dtype=jnp.int32)
    group_of = positions // SEQ
    return (positions % SEQ < SEQ - padding[group_of]).astype(jnp.int32)


def log_spread(key, count, low_end, high_end):
    return jnp.exp(jax.random.uniform(key, (count,), jnp.float32, math.log(low_end), math.log(high_end)))


def draw_moment_router(key, part):
    key = jax.random.fold_in(key, 11)
    value_key, row_key = jax.random.split(key, 2)
    base_scale = 6.0 * TOKENS ** 0.5
    values = jnp.clip(jax.random.normal(value_key, (D, EXPERTS), jnp.float32), -4.0, 4.0)
    row_scales = log_spread(row_key, D, 1.0, 4.0)
    return base_scale * values * row_scales[:, None]


def draw_moment_attention_in(key, part):
    key = jax.random.fold_in(key, 12)
    value_key, row_key = jax.random.split(key, 2)
    base_scale = 6.0 * TOKENS ** 0.5
    values = jnp.clip(jax.random.normal(value_key, (D, 3, HQ), jnp.float32), -4.0, 4.0)
    row_scales = log_spread(row_key, D, 1.0, 4.0)
    return base_scale * values * row_scales[:, None, None]


def block_scale(stream_key, extent, shards, least, largest):
    def one(dim, blocks):
        draws = jax.random.uniform(jax.random.fold_in(jax.random.fold_in(stream_key, 6), dim), (blocks,), jnp.float32, least / len(shards), largest / len(shards))
        return jnp.repeat(jnp.exp(draws), extent[dim] // blocks).reshape((-1,) + (1,) * (len(extent) - dim - 1))

    level = one(*shards[0])
    for cut in shards[1:]:
        level = level * one(*cut)
    return level


def length_profile(number_of, total, reach, slope):
    portions = [(1 << 20) // math.isqrt(standing ** slope) + 1 for standing in range(2, number_of + 1)]
    surplus, given = total - reach - (number_of - 1), [1] * (number_of - 1)
    while surplus > 0:
        movable = [i for i in range(number_of - 1) if given[i] < reach]
        pool, left = sum([portions[i] for i in movable]), surplus
        for i in movable:
            addition = min(reach - given[i], max(1, left * portions[i] // pool), surplus)
            given[i] = given[i] + addition
            surplus = surplus - addition
    return np.array([reach] + given)


def ragged_sizes(rng, number_of, total, bound, skew):
    if number_of == 2:
        one = jax.random.randint(rng, (), max(1, total - bound), min(bound, total - 1) + 1)
        return jnp.stack([one, total - one])
    tallies = jnp.asarray(length_profile(number_of, total, bound, skew), jnp.int32)
    twos = (number_of - 1) // 2
    donor, taker = tallies[1:1 + 2 * twos:2], tallies[2:2 + 2 * twos:2]
    slack = jnp.minimum(donor - 1, bound - taker)
    passed = jax.random.randint(jax.random.fold_in(rng, 1), (twos,), 0, 1 << 20) % (slack + 1)
    tallies = tallies.at[1:1 + 2 * twos:2].set(donor - passed).at[2:2 + 2 * twos:2].set(taker + passed)
    return tallies[jax.random.permutation(jax.random.fold_in(rng, 2), number_of)]


def routed_block(stream_key, own, number, rows, amount, top, reach, skew):
    ranking = jax.random.permutation(stream_key, amount)
    crowded, common = shares(amount, rows * top, reach, skew, True), shares(amount, rows * top, reach, skew, False)
    places = jnp.arange(amount)

    def named(lengths, rotation):
        used = int((lengths > 0).sum())
        fixed = max(1, used // 4)
        passed = fixed + (places - fixed + rotation * (used - fixed)) % max(1, amount - fixed)
        return jnp.zeros((amount,), jnp.int32).at[ranking[jnp.where(places < fixed, places, passed)]].set(jnp.asarray(lengths, jnp.int32))

    lengths = jnp.where(number % 4 == 0, named(crowded, number // 4), named(common, number - number // 4 - 1))
    mixed = jax.random.permutation(jax.random.fold_in(own, 3), amount)
    donor, sink = mixed[0:amount // 2 * 2:2], mixed[1:amount // 2 * 2:2]
    margin = jnp.minimum(lengths[donor] - 1, reach - lengths[sink]) // 2
    margin = jnp.where((donor == ranking[0]) | (sink == ranking[0]) | (lengths[sink] == 0), 0, jnp.maximum(margin, 0))
    passed = jax.random.randint(jax.random.fold_in(own, 4), (amount // 2,), 0, 1 << 20) % (margin + 1)
    lengths = lengths.at[donor].add(-passed).at[sink].add(passed)
    items = jnp.searchsorted(jnp.cumsum(lengths), jnp.arange(rows * top), side="right").astype(jnp.int32)
    listing = items.reshape(top, rows).T
    listing = listing[jax.random.permutation(jax.random.fold_in(own, 1), rows)]
    rotation = jax.random.randint(jax.random.fold_in(own, 2), (rows, 1), 0, top)
    return jnp.take_along_axis(listing, (jnp.arange(top)[None, :] + rotation) % top, axis=1)


def shares(count, total, most, slope, full):
    weights = [(1 << 20) // math.isqrt(standing ** slope) + 1 for standing in range(1, count + 1)]
    largest = most if full else min(most, max(-(-total // count), total * weights[0] // sum(weights)))
    least = 1 if total - largest >= count - 1 else 0
    given, rest = [largest] + [least] * (count - 1), total - largest - least * (count - 1)
    while rest > 0:
        movable = [i for i in range(1, count) if given[i] < largest] or [i for i in range(1, count) if given[i] < most]
        whole, left = sum([weights[i] for i in movable]), rest
        for i in movable:
            more = min(most - given[i], max(1, left * weights[i] // whole), rest)
            given[i] = given[i] + more
            rest = rest - more
    return np.array(given)


def gaussian(stream_key, extent, spread, limit, cuts=(), held_as=jnp.bfloat16):
    gain = block_scale(stream_key, extent, cuts, -0.22, 0.18) if cuts else 1.0
    array = jax.random.normal(stream_key, extent, jnp.float32) * spread * gain
    return jnp.minimum(jnp.maximum(array, -limit), limit).astype(held_as)


def setup_inputs(seed: int = 0) -> dict:
    keys = jax.random.split(jax.random.key(seed), 24)
    tokens = gaussian(keys[0], (TOKENS, D), 1.0, 6.0, ((0, 32),))
    teacher = gaussian(keys[1], (TOKENS, D), 1.0, 6.0, ((0, 32),))
    segments = jnp.searchsorted(jnp.cumsum(ragged_sizes(keys[2], TOKENS * 4 // SEQ, TOKENS, SEQ, 2)), jnp.arange(TOKENS), side="right").astype(jnp.int32)
    valid_mask = draw_valid_mask(jax.random.fold_in(keys[23], 71), 0)
    routes_keys = jax.random.split(jax.random.fold_in(keys[4], 1), TOKENS // SEQ)
    routes_turns = jax.random.permutation(jax.random.fold_in(keys[4], 3), TOKENS // SEQ)
    routes = jax.vmap(lambda own, number: routed_block(jax.random.fold_in(keys[4], 2), own, number, SEQ, EXPERTS, 2, CAP, 2))(routes_keys, routes_turns).reshape((TOKENS, 2))
    first_gain = jnp.clip(1.0 + 0.1 * jax.random.normal(keys[5], (D,), jnp.float32), 0.5, 1.5)
    second_gain = jnp.clip(1.0 + 0.1 * jax.random.normal(keys[6], (D,), jnp.float32), 0.5, 1.5)
    router_weight = gaussian(keys[7], (D, EXPERTS), D ** -0.5, 0.21875, (), jnp.float32)
    attention_in = gaussian(keys[8], (D, 3, HQ), D ** -0.5, 0.21875, ((0, 8), (2, 4)), jnp.float32)
    attention_out = gaussian(keys[9], (D, HQ), (HQ // 32) ** -0.5, 1.25, ((0, 8), (1, 4)), jnp.float32)
    dense_in = gaussian(keys[10], (D, 2, FF), D ** -0.5, 0.21875, ((0, 8), (2, 4)), jnp.float32)
    dense_out = gaussian(keys[11], (D, FF), FF ** -0.5, 0.125, ((0, 8), (1, 4)), jnp.float32)
    expert_in = gaussian(keys[12], (EXPERTS * EQ, D, 2, FF // EQ), D ** -0.5, 0.21875, ((0, 8), (3, 4)), jnp.float32)
    expert_out = gaussian(keys[13], (EXPERTS * EQ, D, FF // EQ), FF ** -0.5, 0.125, ((0, 8), (2, 4)), jnp.float32)
    moment_first_gain = gaussian(keys[14], (D,), (0.5 * TOKENS ** 0.5), 192.0, (), jnp.float32)
    moment_second_gain = gaussian(keys[15], (D,), (0.5 * TOKENS ** 0.5), 192.0, (), jnp.float32)
    moment_router = draw_moment_router(jax.random.fold_in(keys[23], 71), 0)
    moment_attention_in = draw_moment_attention_in(jax.random.fold_in(keys[23], 71), 0)
    moment_attention_out = gaussian(keys[18], (D, HQ), (0.2 * TOKENS ** 0.5), 80.0, ((0, 8), (1, 4)), jnp.float32)
    moment_dense_in = gaussian(keys[19], (D, 2, FF), (0.2 * TOKENS ** 0.5), 80.0, ((0, 8), (2, 4)), jnp.float32)
    moment_dense_out = gaussian(keys[20], (D, FF), (0.2 * TOKENS ** 0.5), 80.0, ((0, 8), (1, 4)), jnp.float32)
    moment_expert_in = gaussian(keys[21], (EXPERTS * EQ, D, 2, FF // EQ), (0.1 * (TOKENS * 2 // EXPERTS) ** 0.5), 14.0, ((0, 8), (3, 4)), jnp.float32)
    moment_expert_out = gaussian(keys[22], (EXPERTS * EQ, D, FF // EQ), (0.1 * (TOKENS * 2 // EXPERTS) ** 0.5), 14.0, ((0, 8), (2, 4)), jnp.float32)
    return {"tokens": tokens, "teacher": teacher, "segments": segments, "valid_mask": valid_mask, "routes": routes, "first_gain": first_gain, "second_gain": second_gain, "router_weight": router_weight, "attention_in": attention_in, "attention_out": attention_out, "dense_in": dense_in, "dense_out": dense_out, "expert_in": expert_in, "expert_out": expert_out, "moment_first_gain": moment_first_gain, "moment_second_gain": moment_second_gain, "moment_router": moment_router, "moment_attention_in": moment_attention_in, "moment_attention_out": moment_attention_out, "moment_dense_in": moment_dense_in, "moment_dense_out": moment_dense_out, "moment_expert_in": moment_expert_in, "moment_expert_out": moment_expert_out}


@jax.custom_vjp
def low(v):
    return lax.optimization_barrier(v.astype(jnp.bfloat16)).astype(jnp.float32)

@jax.custom_vjp
def low_back(v):
    return v

def low_keep(v):
    return (low(v), None)

def low_pass(kept, grad):
    return (grad,)

def back_keep(v):
    return (v, None)

def back_low(kept, grad):
    return (low(grad),)
low.defvjp(low_keep, low_pass)
low_back.defvjp(back_keep, back_low)
highest = lax.Precision.HIGHEST
norm_eps = 1e-06
rope_base = 10000.0
masked_score = -1e+30
ns_first = 3.4445
ns_second = -4.775
ns_third = 2.0315
decay_rate = 0.5
gain_rate = 0.05
router_rate = 0.02

def matmul(left, right):
    return jnp.dot(left, right, precision=highest)

def rms_scale(values):
    return lax.rsqrt(lax.optimization_barrier(jnp.mean(values * values, axis=-1, keepdims=True)) + norm_eps)

def rotate(values, positions, direction):
    half_dim = values.shape[-1] // 2
    frequency = rope_base ** (-jnp.arange(half_dim).astype(jnp.float32) * 2.0 / values.shape[-1])
    angles = positions[:, None] * frequency[None, :]
    cosine = jnp.cos(angles)[:, None, :]
    sine_part = direction * jnp.sin(angles)[:, None, :]
    first_half = values[..., :half_dim]
    second = values[..., half_dim:]
    return jnp.concatenate([first_half * cosine - second * sine_part, second * cosine + first_half * sine_part], axis=-1)

def slot_tables(route_rows):
    flat_routes = route_rows.reshape(-1).astype(jnp.int32)
    assign_count = flat_routes.shape[0]
    sort_order = jnp.argsort(flat_routes, stable=True).astype(jnp.int32)
    onehot = (flat_routes[:, None] == jnp.arange(EXPERTS, dtype=jnp.int32)[None, :]).astype(jnp.int32)
    counts = lax.optimization_barrier(jnp.sum(onehot, axis=0)).astype(jnp.int32)
    starts = (jnp.cumsum(counts) - counts).astype(jnp.int32)
    sorted_ranks = jnp.arange(assign_count, dtype=jnp.int32) - starts[flat_routes[sort_order]]
    slot_ranks = jnp.zeros((assign_count,), jnp.int32).at[sort_order].set(sorted_ranks.astype(jnp.int32))
    slot_ids = (flat_routes * CAP + slot_ranks).astype(jnp.int32)
    source = jnp.full((EXPERTS * CAP,), -1, jnp.int32).at[slot_ids].set(jnp.arange(assign_count, dtype=jnp.int32))
    return (slot_ids, source)

def group_forward(params, group_data):
    first_gain, second_gain, router_weight, attention_in, attention_out, dense_in, dense_out, expert_in, expert_out = params
    tokens, teacher, segments, valid_mask, routes = group_data
    seq_len = tokens.shape[0]
    normed_one = low(tokens * rms_scale(tokens) * first_gain)
    projected = low_back(matmul(normed_one, low(attention_in).reshape(D, 3 * HQ))).reshape(seq_len, 3, HEADS, HEAD_DIM)
    positions = jnp.arange(seq_len).astype(jnp.float32)
    queries = low(rotate(projected[:, 0], positions, 1.0) * HEAD_DIM ** (-0.5))
    key_rows = low(rotate(projected[:, 1], positions, 1.0))
    value_rows = low(projected[:, 2])
    scores = low_back(jnp.einsum('qhd,khd->hqk', queries, key_rows, precision=highest))
    index_rows = jnp.arange(seq_len)
    allowed = (segments[:, None] == segments[None, :]) & (index_rows[:, None] >= index_rows[None, :])
    scores = jnp.where(allowed[None], scores, masked_score)
    score_weights = jax.nn.softmax(scores, axis=-1)
    mixed_heads = jnp.einsum('hqk,khd->qhd', low(score_weights), value_rows, precision=highest)
    mixed_heads = low_back(low(mixed_heads)).reshape(seq_len, HQ)
    attended = low_back(matmul(mixed_heads, low(attention_out).T))
    hidden = tokens + attended
    normed_two = low(hidden * rms_scale(hidden) * second_gain)
    gate_up = low_back(matmul(normed_two, low(dense_in).reshape(D, 2 * FF))).reshape(seq_len, 2, FF)
    dense_inner = low(jax.nn.silu(gate_up[:, 0]) * gate_up[:, 1])
    dense_part = matmul(dense_inner, low(dense_out).T)
    logits = matmul(normed_two, low(router_weight))
    onehot = routes[:, :, None] == jnp.arange(EXPERTS, dtype=jnp.int32)[None, None, :]
    chosen = lax.optimization_barrier(jnp.sum(jnp.where(onehot, logits[:, None, :], 0.0), axis=-1))
    gate_probs = jax.nn.softmax(chosen, axis=-1)
    slot_ids, source = slot_tables(routes)
    filled = source >= 0
    dispatched = jnp.where(filled[:, None], normed_two[jnp.maximum(source, 0) // 2], 0.0)
    slot_inputs = dispatched.reshape(EXPERTS, CAP, D)
    block_count = EQ * N_MP
    block_width = FF // block_count
    weight_in = low(expert_in).reshape(EXPERTS, EQ, D, 2, N_MP, block_width).transpose(0, 2, 3, 1, 4, 5).reshape(EXPERTS, D, 2, block_count, block_width)
    weight_out = low(expert_out).reshape(EXPERTS, EQ, D, N_MP, block_width).transpose(0, 2, 1, 3, 4).reshape(EXPERTS, D, block_count, block_width)
    expert_sum = jnp.zeros((EXPERTS, CAP, D), jnp.float32)
    for part_index in range(block_count):
        block_inputs = low_back(slot_inputs)
        block_gate_up = low_back(jnp.einsum('ecd,edgf->ecgf', block_inputs, weight_in[:, :, :, part_index], precision=highest))
        block_inner = low(jax.nn.silu(block_gate_up[:, :, 0]) * block_gate_up[:, :, 1])
        expert_sum = expert_sum + low(jnp.einsum('ecf,edf->ecd', block_inner, weight_out[:, :, part_index], precision=highest))
    expert_rows = low_back(expert_sum).reshape(EXPERTS * CAP, D)
    picked = expert_rows[slot_ids].reshape(seq_len, 2, D)
    mixture = lax.optimization_barrier(jnp.sum(gate_probs[:, :, None] * picked, axis=1))
    branch = low_back(dense_part + mixture)
    output = hidden + branch
    errors = output - teacher
    loss_sum = jnp.sum(lax.optimization_barrier(jnp.sum(errors * errors, axis=-1)) * valid_mask)
    return (output, loss_sum)

def split_columns(matrix, parts, block_count):
    columns = matrix.shape[-1] // block_count
    return matrix.reshape(D, parts, block_count, columns).transpose(0, 2, 1, 3).reshape(D, block_count, parts * columns)

def join_columns(blocks, parts):
    block_count = blocks.shape[1]
    columns = blocks.shape[-1] // parts
    return blocks.reshape(D, block_count, parts, columns).transpose(0, 2, 1, 3).reshape(D, parts, block_count * columns)

def orthogonalize(blocks):
    rounded = low(blocks)
    squares = jnp.sum(rounded * rounded)
    current = low(rounded * lax.rsqrt(squares + 1e-12))
    iterate = current
    for iteration in range(NS_ITERS):
        gram_total = lax.optimization_barrier(jnp.sum(low(jnp.einsum('dbc,ebc->bde', current, current, precision=highest)), axis=0))
        gram_low = low(gram_total)
        square = matmul(gram_low, gram_low)
        polynomial = low(ns_second * gram_total + ns_third * square)
        iterate = ns_first * current + jnp.einsum('de,ebc->dbc', polynomial, current, precision=highest)
        current = low(iterate)
    return iterate

def muon_delta(moment, parts, block_count):
    shaped = moment.reshape(D, parts, -1)
    step_scale = (shaped.shape[1] * shaped.shape[2] / D) ** 0.5
    result = join_columns(orthogonalize(split_columns(shaped, parts, block_count)), parts)
    return -step_scale * result.reshape(moment.shape)

def muon_step(weight, moment, parts, block_count):
    return weight + muon_delta(moment, parts, block_count)

def normed_delta(moment, step_rate):
    return -step_rate * moment * lax.rsqrt(jnp.mean(moment * moment) + 1e-12)

def reference(tokens, teacher, segments, valid_mask, routes, first_gain, second_gain, router_weight, attention_in, attention_out, dense_in, dense_out, expert_in, expert_out, moment_first_gain, moment_second_gain, moment_router, moment_attention_in, moment_attention_out, moment_dense_in, moment_dense_out, moment_expert_in, moment_expert_out):
    params = tuple((weight_item.astype(jnp.float32) for weight_item in (first_gain, second_gain, router_weight, attention_in, attention_out, dense_in, dense_out, expert_in, expert_out)))
    groups = TOKENS // SEQ
    tokens_float = tokens.astype(jnp.float32)
    teacher_grouped = teacher.astype(jnp.float32).reshape(groups, SEQ, D)
    mask_float = valid_mask.astype(jnp.float32)
    valid_count = jnp.sum(mask_float)
    checked = jax.checkpoint(group_forward)

    def objective(weights, inputs):

        def one_group(running, group_data):
            group_out, group_loss = checked(weights, group_data)
            return (running + group_loss, group_out)
        loss_total, outputs = lax.scan(one_group, jnp.zeros((), jnp.float32), (inputs.reshape(groups, SEQ, D), teacher_grouped, segments.reshape(groups, SEQ), mask_float.reshape(groups, SEQ), routes.reshape(groups, SEQ, 2)))
        return (outputs.reshape(TOKENS, D), loss_total / (valid_count * D))
    (output, loss_value), pullback = jax.vjp(objective, params, tokens_float)
    grad_params, grad_tokens = pullback((jnp.zeros_like(output), jnp.ones_like(loss_value) * (TOKENS * D / 2)))
    moments = (moment_first_gain, moment_second_gain, moment_router, moment_attention_in, moment_attention_out, moment_dense_in, moment_dense_out, moment_expert_in, moment_expert_out)
    new_moments = tuple((decay_rate * moment_item + grad_item for moment_item, grad_item in zip(moments, grad_params)))
    step_first = normed_delta(new_moments[0], gain_rate)
    step_second = normed_delta(new_moments[1], gain_rate)
    new_router = params[2] + normed_delta(new_moments[2], router_rate)
    new_attention_in = muon_step(params[3], new_moments[3], 3, N_MP)
    step_attention_out = muon_delta(new_moments[4], 1, N_MP)
    new_dense_in = muon_step(params[5], new_moments[5], 2, N_MP)
    new_dense_out = muon_step(params[6], new_moments[6], 1, N_MP)

    def expert_in_step(pair_items):
        return muon_step(pair_items[0], pair_items[1], 2, N_MP)

    def expert_out_step(pair_items):
        return muon_step(pair_items[0], pair_items[1], 1, N_MP)
    new_expert_in = lax.map(expert_in_step, (params[7], new_moments[7]))
    new_expert_out = lax.map(expert_out_step, (params[8], new_moments[8]))
    return (output.astype(jnp.bfloat16), loss_value, grad_tokens, grad_params[0], grad_params[1], grad_params[2], grad_params[3], grad_params[4], grad_params[5], grad_params[6], grad_params[7], grad_params[8], new_moments[0], new_moments[1], new_moments[2], new_moments[3], new_moments[4], new_moments[5], new_moments[6], new_moments[7], new_moments[8], step_first, step_second, new_router, new_attention_in, step_attention_out, new_dense_in, new_dense_out, new_expert_in, new_expert_out)
```

```python
import jax
import jax.numpy as jnp
from jax import lax
from jax.sharding import Mesh
from jax.sharding import PartitionSpec as P

D = 768
HEADS = 12
HEAD_DIM = 64
FF = 2048

highest = lax.Precision.HIGHEST
bf16 = jnp.bfloat16
f32 = jnp.float32
norm_eps = 1e-06
rope_base = 10000.0
masked_score = -1e30
ns_first = 3.4445
ns_second = -4.775
ns_third = 2.0315
decay_rate = 0.5
gain_rate = 0.05
router_rate = 0.02

DP = ("z", "y")
MP = ("x", "c")
SPARE = 64


def rms_scale(values):
    return lax.rsqrt(jnp.mean(values * values, axis=-1, keepdims=True) + norm_eps)


def rotate(values, cosine, sine_part):
    half_dim = values.shape[-1] // 2
    first_half = values[..., :half_dim]
    second = values[..., half_dim:]
    return jnp.concatenate(
        [first_half * cosine - second * sine_part, second * cosine + first_half * sine_part],
        axis=-1,
    )


def swiglu_back(gate_values, up_values, grad_inner):
    sigmoid_gate = jax.nn.sigmoid(gate_values)
    grad_gate_part = (
        grad_inner * up_values * sigmoid_gate * (1.0 + gate_values * (1.0 - sigmoid_gate))
    )
    grad_up_part = grad_inner * gate_values * sigmoid_gate
    return grad_gate_part.astype(bf16), grad_up_part.astype(bf16)


def norm_back(grad_normed, inputs, row_scale, norm_gain):
    scaled = grad_normed * norm_gain
    return row_scale * scaled - inputs * row_scale**3 * jnp.mean(
        scaled * inputs, axis=-1, keepdims=True
    )


def mm(left, right):
    return jnp.dot(left, right, preferred_element_type=f32)


def mm_t(left, right):
    return lax.dot_general(left, right, (((1,), (1,)), ((), ())), preferred_element_type=f32)


def t_mm(left, right):
    return lax.dot_general(left, right, (((0,), (0,)), ((), ())), preferred_element_type=f32)


def gather_rows(values):
    return lax.all_gather(values, MP, axis=0, tiled=True)


def scatter_rows(values):
    parts = lax.all_to_all(values.astype(bf16), MP, split_axis=0, concat_axis=0, tiled=True)
    return jnp.sum(parts.reshape(lax.axis_size(MP), -1, values.shape[1]).astype(f32), axis=0)


def gather_shards(values):
    paired = lax.all_gather(values, "y", axis=0, tiled=True)
    return lax.all_gather(paired, "z", axis=0, tiled=True)


def scatter_shards(values):
    parts = lax.all_to_all(values.astype(bf16), DP, split_axis=0, concat_axis=0, tiled=True)
    return jnp.sum(parts.reshape(lax.axis_size(DP), -1, values.shape[1]).astype(f32), axis=0)


def exchange(values):
    return lax.all_to_all(values, DP, split_axis=0, concat_axis=0, tiled=True)


def gram_term(matrix):
    return mm_t(matrix, matrix).astype(bf16)


def bmm(left, right):
    return jnp.einsum("nij,njk->nik", left, right, preferred_element_type=f32)


def step_matrices(grams):
    inverse = 1.0 / (jnp.trace(grams, axis1=1, axis2=2) + 1e-12)
    first_gram = grams * inverse[:, None, None]
    first_low = first_gram.astype(bf16)
    first_poly = (ns_second * first_gram + ns_third * bmm(first_low, first_low)).astype(bf16)
    mixed = bmm(first_poly, first_low)
    second_gram = (
        ns_first * ns_first * first_gram
        + 2.0 * ns_first * mixed
        + bmm(mixed.astype(bf16), first_poly)
    )
    second_low = second_gram.astype(bf16)
    second_poly = (ns_second * second_gram + ns_third * bmm(second_low, second_low)).astype(bf16)
    combined = ns_first * (first_poly.astype(f32) + second_poly.astype(f32)) + bmm(
        second_poly, first_poly
    )
    return combined.astype(bf16), inverse


def normed_delta(moment, step_rate):
    return -step_rate * moment * lax.rsqrt(jnp.mean(moment * moment) + 1e-12)


def local(
    tokens,
    teacher,
    segments,
    valid_mask,
    routes,
    first_gain,
    second_gain,
    router_weight,
    attention_in,
    attention_out,
    dense_in,
    dense_out,
    expert_in,
    expert_out,
    moment_first_gain,
    moment_second_gain,
    moment_router,
    moment_attention_in,
    moment_attention_out,
    moment_dense_in,
    moment_dense_out,
    moment_expert_in,
    moment_expert_out,
):
    row_count, width = tokens.shape
    mp_ways = lax.axis_size(MP)
    dp_ways = lax.axis_size(DP)
    mp_place = lax.axis_index(MP)
    dp_place = lax.axis_index(DP)
    core_place = lax.axis_index("c")
    seq_len = row_count * mp_ways
    expert_total = router_weight.shape[1]
    capacity = 4 * seq_len // expert_total
    half_cap = capacity // 2
    shard_rows = attention_in.shape[0]
    slabs = expert_in.shape[0]
    units = expert_in.shape[3]
    dense_units = dense_in.shape[2]
    sharing = FF // (units * mp_ways)
    heads_here = attention_in.shape[2] // HEAD_DIM
    head_cols = attention_in.shape[2]
    project_cols = 3 * head_cols
    project_scale = (3 * HEADS * HEAD_DIM / D) ** 0.5
    mix_scale = (HEADS * HEAD_DIM / D) ** 0.5
    pair_scale = (2 * FF / D) ** 0.5
    single_scale = (FF / D) ** 0.5
    slab_pair_scale = (2 * FF / (sharing * D)) ** 0.5
    slab_single_scale = (FF / (sharing * D)) ** 0.5

    mask_float = valid_mask.astype(f32)
    own_count = jnp.sum(mask_float)
    high_count = jnp.floor(own_count / 256.0)
    count_cells = jnp.zeros((shard_rows, SPARE), f32)
    count_cells = count_cells.at[0, 0].set(high_count)
    count_cells = count_cells.at[1, 0].set(own_count - 256.0 * high_count)
    first_pack = jnp.concatenate(
        [attention_in.reshape(shard_rows, project_cols), count_cells], axis=1
    ).astype(bf16)
    first_full = gather_shards(first_pack)
    weight_project = first_full[:, :project_cols]
    counts = first_full[:, project_cols].astype(f32).reshape(dp_ways, shard_rows)
    valid_count = jnp.sum(256.0 * counts[:, 0] + counts[:, 1])
    weight_mix = gather_shards(attention_out.astype(bf16))
    second_pack = jnp.concatenate(
        [dense_in[:, 0, :], dense_in[:, 1, :], dense_out], axis=1
    ).astype(bf16)
    second_full = lax.all_gather(second_pack, DP, axis=0, tiled=True)
    weight_pair = second_full[:, : 2 * dense_units]
    weight_down = second_full[:, 2 * dense_units :]
    router_low = router_weight.astype(bf16)
    expert_gate = expert_in[:, :, 0, :].astype(bf16)
    expert_up = expert_in[:, :, 1, :].astype(bf16)
    expert_down = expert_out.astype(bf16)

    onehot = (
        routes[:, :, None] == jnp.arange(expert_total, dtype=jnp.int32)[None, None, :]
    ).astype(f32)
    order = jnp.arange(seq_len, dtype=jnp.int32)
    earlier = mm(
        (order[:, None] > order[None, :]).astype(bf16), jnp.sum(onehot, axis=1).astype(bf16)
    )
    ranks = jnp.sum(onehot * earlier[:, None, :], axis=-1).astype(jnp.int32)
    half_ranks = ranks - core_place * half_cap
    here = (half_ranks >= 0) & (half_ranks < half_cap)
    slot_ids = jnp.where(here, routes * half_cap + half_ranks, -1)
    slot_total = expert_total * half_cap
    slot_order = jnp.arange(slot_total, dtype=jnp.int32)
    picks = [(slot_ids[:, k][:, None] == slot_order[None, :]) for k in range(2)]
    select = (picks[0] | picks[1]).astype(bf16)

    token_float = tokens.astype(f32)
    scale_one = rms_scale(token_float)
    full_one = gather_rows((token_float * scale_one * first_gain).astype(bf16))
    projected = mm(full_one, weight_project).reshape(seq_len, 3, heads_here, HEAD_DIM)
    positions = jnp.arange(seq_len, dtype=f32)
    frequency = rope_base ** (-jnp.arange(HEAD_DIM // 2, dtype=f32) * 2.0 / HEAD_DIM)
    angles = positions[:, None] * frequency[None, :]
    cosine = jnp.cos(angles)[:, None, :]
    sine = jnp.sin(angles)[:, None, :]
    query_scale = HEAD_DIM ** (-0.5)
    queries = (rotate(projected[:, 0], cosine, sine) * query_scale).astype(bf16)
    key_rows = rotate(projected[:, 1], cosine, sine).astype(bf16)
    value_rows = projected[:, 2].astype(bf16)
    allowed = (segments[:, None] == segments[None, :]) & (order[:, None] >= order[None, :])

    def head_scores():
        scores = jnp.einsum("qhd,khd->hqk", queries, key_rows, preferred_element_type=f32)
        return jnp.where(allowed[None], scores, masked_score)

    scores = head_scores()
    row_peak = jnp.max(scores, axis=-1, keepdims=True)
    exponent = jnp.exp(scores - row_peak)
    row_total = jnp.sum(exponent, axis=-1, keepdims=True)
    probs = exponent / row_total
    probs_low = probs.astype(bf16)
    mixed_low = (
        jnp.einsum("hqk,khd->qhd", probs_low, value_rows, preferred_element_type=f32)
        .astype(bf16)
        .reshape(seq_len, head_cols)
    )
    log_totals = row_peak + jnp.log(row_total)
    attended = scatter_rows(mm_t(mixed_low, weight_mix))
    hidden = token_float + attended
    scale_two = rms_scale(hidden)
    full_two = gather_rows((hidden * scale_two * second_gain).astype(bf16))

    dispatched = t_mm(select, full_two).astype(bf16)

    def to_owners(rows):
        spread = jnp.broadcast_to(
            rows.reshape(expert_total, 1, half_cap, width),
            (expert_total, sharing, half_cap, width),
        ).reshape(expert_total * sharing, half_cap, width)
        moved = exchange(spread).reshape(dp_ways, slabs, half_cap, width)
        both = lax.all_gather(moved, "c", axis=0)
        return [both[:, :, slab].reshape(-1, width) for slab in range(slabs)]

    def to_sources(parts):
        stacked = jnp.stack(
            [part.reshape(2, dp_ways, half_cap, width) for part in parts], axis=2
        )
        swapped = lax.all_to_all(stacked, "c", split_axis=0, concat_axis=0, tiled=True)
        halves = (swapped[0].astype(f32) + swapped[1].astype(f32)).astype(bf16)
        moved = exchange(halves.reshape(dp_ways * slabs, half_cap, width))
        moved = moved.reshape(expert_total, sharing, half_cap, width)
        if sharing > 1:
            moved = jnp.sum(moved.astype(f32), axis=1).astype(bf16)
        return moved.reshape(slot_total, width)

    received = to_owners(dispatched)

    gate_up = mm(full_two, weight_pair)
    gate_part = gate_up[:, :dense_units]
    up_part = gate_up[:, dense_units:]
    dense_inner = (jax.nn.silu(gate_part) * up_part).astype(bf16)
    dense_part = mm_t(dense_inner, weight_down)
    logits = mm(full_two, router_low)
    chosen = jnp.sum(onehot * logits[:, None, :], axis=-1)
    gate_probs = jax.nn.softmax(chosen, axis=-1)
    weighted = (
        jnp.where(picks[0], gate_probs[:, 0:1], 0.0) + jnp.where(picks[1], gate_probs[:, 1:2], 0.0)
    ).astype(bf16)

    slab_gate, slab_up, slab_inner, slab_parts = [], [], [], []
    for slab in range(slabs):
        gate_values = mm(received[slab], expert_gate[slab])
        up_values = mm(received[slab], expert_up[slab])
        inner = (jax.nn.silu(gate_values) * up_values).astype(bf16)
        slab_gate.append(gate_values)
        slab_up.append(up_values)
        slab_inner.append(inner)
        slab_parts.append(mm_t(inner, expert_down[slab]).astype(bf16))
    expert_rows = to_sources(slab_parts)
    branch = scatter_rows(dense_part + mm(weighted, expert_rows))
    output = hidden + branch
    errors = output - teacher.astype(f32)
    own_mask = lax.dynamic_slice_in_dim(mask_float, mp_place * row_count, row_count, 0)
    loss_local = jnp.sum(jnp.sum(errors * errors, axis=-1) * own_mask)
    factor = seq_len * dp_ways / valid_count
    grad_output = errors * (own_mask * factor)[:, None]
    grad_branch = gather_rows(grad_output.astype(bf16))

    raw_slots = t_mm(select, grad_branch)
    slot_gates = jnp.sum(
        jnp.where(picks[0], gate_probs[:, 0:1], 0.0) + jnp.where(picks[1], gate_probs[:, 1:2], 0.0),
        axis=0,
    )
    grad_slots = (raw_slots * slot_gates[:, None]).astype(bf16)
    grad_received = to_owners(grad_slots)
    slot_dots = jnp.sum(raw_slots * expert_rows.astype(f32), axis=-1)
    grad_chosen_raw = jnp.stack(
        [jnp.sum(jnp.where(pick, slot_dots[None, :], 0.0), axis=-1) for pick in picks], axis=-1
    )
    grad_chosen = gate_probs * (
        grad_chosen_raw - jnp.sum(gate_probs * grad_chosen_raw, axis=-1, keepdims=True)
    )
    grad_logits = jnp.sum(onehot * grad_chosen[:, :, None], axis=1)
    logits_high = grad_logits.astype(bf16)
    logits_rest = (grad_logits - logits_high.astype(f32)).astype(bf16)
    grad_router = t_mm(full_two, logits_high) + t_mm(full_two, logits_rest)

    grad_dense_inner = mm(grad_branch, weight_down)
    grad_gate, grad_up = swiglu_back(gate_part, up_part, grad_dense_inner)
    grad_pair = jnp.concatenate([grad_gate, grad_up], axis=1)
    grad_down = t_mm(grad_branch, dense_inner)
    grad_dense_in = t_mm(full_two, grad_pair)
    grad_full_two = (
        mm_t(grad_pair, weight_pair) + mm_t(logits_high, router_low) + mm_t(logits_rest, router_low)
    )
    dense_shard = scatter_shards(jnp.concatenate([grad_dense_in, grad_down], axis=1))

    slab_dispatch, grad_expert_gate, grad_expert_up, grad_expert_down = [], [], [], []
    for slab in range(slabs):
        grad_inner = mm(grad_received[slab], expert_down[slab])
        grad_g, grad_u = swiglu_back(slab_gate[slab], slab_up[slab], grad_inner)
        slab_dispatch.append(
            (mm_t(grad_g, expert_gate[slab]) + mm_t(grad_u, expert_up[slab])).astype(bf16)
        )
        grad_expert_gate.append(t_mm(received[slab], grad_g))
        grad_expert_up.append(t_mm(received[slab], grad_u))
        grad_expert_down.append(t_mm(grad_received[slab], slab_inner[slab]))
    grad_slot_rows = to_sources(slab_dispatch)
    grad_normed_two = scatter_rows(grad_full_two + mm(select, grad_slot_rows))

    grad_expert_in = jnp.stack(
        [
            jnp.stack([grad_expert_gate[slab], grad_expert_up[slab]], axis=1)
            for slab in range(slabs)
        ]
    )
    grad_expert_out = jnp.stack(grad_expert_down)
    new_moment_expert_in = decay_rate * moment_expert_in + grad_expert_in
    new_moment_expert_out = decay_rate * moment_expert_out + grad_expert_out
    shard_pair = dense_shard[:, : 2 * dense_units].reshape(shard_rows, 2, dense_units)
    shard_down = dense_shard[:, 2 * dense_units :]
    new_moment_pair = decay_rate * moment_dense_in + shard_pair
    new_moment_down = decay_rate * moment_dense_out + shard_down
    dense_moments = lax.all_gather(
        jnp.concatenate(
            [new_moment_pair[:, 0, :], new_moment_pair[:, 1, :], new_moment_down], axis=1
        ).astype(bf16),
        DP,
        axis=0,
        tiled=True,
    )
    full_pair = dense_moments[:, : 2 * dense_units]
    full_down = dense_moments[:, 2 * dense_units :]
    early = [full_pair, full_down]
    for slab in range(slabs):
        early.append(
            jnp.concatenate(
                [new_moment_expert_in[slab, :, 0, :], new_moment_expert_in[slab, :, 1, :]], axis=1
            ).astype(bf16)
        )
        early.append(new_moment_expert_out[slab].astype(bf16))
    early_grams = lax.psum(jnp.stack([gram_term(matrix) for matrix in early]), MP)
    share = len(early) // 2
    own_grams = lax.dynamic_slice_in_dim(early_grams, core_place * share, share, 0).astype(f32)
    own_steps, own_inverse = step_matrices(own_grams)
    early_steps = lax.all_gather(own_steps, "c", axis=0, tiled=True)
    early_inverse = lax.all_gather(own_inverse, "c", axis=0, tiled=True)

    grad_hidden = norm_back(grad_normed_two, hidden, scale_two, second_gain) + grad_output
    grad_second_part = jnp.sum(grad_normed_two * hidden * scale_two, axis=0)
    grad_attended = gather_rows(grad_hidden.astype(bf16))
    grad_mix = t_mm(grad_attended, mixed_low)
    grad_mixed = (
        mm(grad_attended, weight_mix).astype(bf16).reshape(seq_len, heads_here, HEAD_DIM)
    )
    score_weights = jnp.exp(head_scores() - log_totals)
    grad_weights = jnp.einsum("qhd,khd->hqk", grad_mixed, value_rows, preferred_element_type=f32)
    row_dots = jnp.sum(grad_weights * score_weights, axis=-1, keepdims=True)
    grad_scores = (score_weights * (grad_weights - row_dots)).astype(bf16)
    grad_queries = jnp.einsum("hqk,khd->qhd", grad_scores, key_rows, preferred_element_type=f32)
    grad_keys = jnp.einsum("hqk,qhd->khd", grad_scores, queries, preferred_element_type=f32)
    grad_values = jnp.einsum(
        "hqk,qhd->khd", score_weights.astype(bf16), grad_mixed, preferred_element_type=f32
    )
    grad_projected = jnp.concatenate(
        [
            rotate(grad_queries * query_scale, cosine, -sine).reshape(seq_len, head_cols),
            rotate(grad_keys, cosine, -sine).reshape(seq_len, head_cols),
            grad_values.reshape(seq_len, head_cols),
        ],
        axis=1,
    ).astype(bf16)
    grad_project = t_mm(full_one, grad_projected)
    grad_full_one = mm_t(grad_projected, weight_project)
    grad_first_part = jnp.sum(grad_full_one * full_one.astype(f32), axis=0) / first_gain

    loss_cells = jnp.zeros((width, 1), f32).at[0, 0].set(loss_local)
    small = jnp.concatenate(
        [grad_first_part[:, None], grad_second_part[:, None], grad_router, loss_cells], axis=1
    )
    small = jnp.pad(small, ((0, 0), (0, SPARE - small.shape[1])))
    mix_shard = scatter_shards(grad_mix)
    new_moment_mix = decay_rate * moment_attention_out + mix_shard
    last_shard = scatter_shards(jnp.concatenate([grad_project, small], axis=1))
    shard_project = last_shard[:, :project_cols].reshape(shard_rows, 3, head_cols)
    new_moment_project = decay_rate * moment_attention_in + shard_project
    last_moments = gather_shards(
        jnp.concatenate(
            [
                new_moment_project.reshape(shard_rows, project_cols),
                last_shard[:, project_cols:],
                new_moment_mix,
            ],
            axis=1,
        ).astype(bf16)
    )
    full_project = last_moments[:, :project_cols]
    full_mix = last_moments[:, project_cols + SPARE :]
    last_sums = lax.all_to_all(
        jnp.concatenate(
            [
                gram_term(full_project),
                gram_term(full_mix),
                last_moments[:, project_cols : project_cols + SPARE],
            ],
            axis=1,
        ),
        MP,
        split_axis=0,
        concat_axis=0,
        tiled=True,
    )
    last_sums = jnp.sum(last_sums.reshape(mp_ways, -1, last_sums.shape[1]).astype(f32), axis=0)
    last_sums = gather_rows(last_sums.astype(bf16))
    last_steps, last_inverse = step_matrices(
        jnp.stack([last_sums[:, :width], last_sums[:, width : 2 * width]]).astype(f32)
    )
    small_total = last_sums[:, 2 * width :].astype(f32)
    grad_normed_one = scatter_rows(grad_full_one)
    grad_tokens = norm_back(grad_normed_one, token_float, scale_one, first_gain) + grad_hidden

    first_total = small_total[:, 0]
    second_total = small_total[:, 1]
    router_total = small_total[:, 2 : 2 + expert_total]
    loss_total = small_total[0, 2 + expert_total]
    loss_value = loss_total / (valid_count * width)
    new_moment_first = decay_rate * moment_first_gain + first_total
    new_moment_second = decay_rate * moment_second_gain + second_total
    new_moment_router = decay_rate * moment_router + router_total

    def update(step, inverse, matrix, step_scale):
        full = ns_first * ns_first * matrix.astype(f32) + mm(step, matrix)
        return (-step_scale * jnp.sqrt(inverse)) * full

    def update_rows(step, inverse, matrix, step_scale):
        step_rows = lax.dynamic_slice_in_dim(step, dp_place * shard_rows, shard_rows, 0)
        own_rows = lax.dynamic_slice_in_dim(matrix, dp_place * shard_rows, shard_rows, 0)
        full = ns_first * ns_first * own_rows.astype(f32) + mm(step_rows, matrix)
        return (-step_scale * jnp.sqrt(inverse)) * full

    step_first = normed_delta(new_moment_first, gain_rate)
    step_second = normed_delta(new_moment_second, gain_rate)
    new_router = router_weight + normed_delta(new_moment_router, router_rate)
    new_attention_in = attention_in + update_rows(
        last_steps[0], last_inverse[0], full_project, project_scale
    ).reshape(attention_in.shape)
    step_mix = update_rows(last_steps[1], last_inverse[1], full_mix, mix_scale)
    new_dense_in = dense_in + update_rows(
        early_steps[0], early_inverse[0], full_pair, pair_scale
    ).reshape(dense_in.shape)
    new_dense_out = dense_out + update_rows(
        early_steps[1], early_inverse[1], full_down, single_scale
    )
    pair_steps, single_steps = [], []
    for slab in range(slabs):
        place = 2 + 2 * slab
        pair_steps.append(
            update(early_steps[place], early_inverse[place], early[place], slab_pair_scale).reshape(
                width, 2, units
            )
        )
        single_steps.append(
            update(
                early_steps[place + 1],
                early_inverse[place + 1],
                early[place + 1],
                slab_single_scale,
            )
        )
    new_expert_in = expert_in + jnp.stack(pair_steps)
    new_expert_out = expert_out + jnp.stack(single_steps)
    return (
        output.astype(bf16),
        loss_value,
        grad_tokens,
        first_total,
        second_total,
        router_total,
        shard_project,
        mix_shard,
        shard_pair,
        shard_down,
        grad_expert_in,
        grad_expert_out,
        new_moment_first,
        new_moment_second,
        new_moment_router,
        new_moment_project,
        new_moment_mix,
        new_moment_pair,
        new_moment_down,
        new_moment_expert_in,
        new_moment_expert_out,
        step_first,
        step_second,
        new_router,
        new_attention_in,
        step_mix,
        new_dense_in,
        new_dense_out,
        new_expert_in,
        new_expert_out,
    )


def solution(mesh):
    dp_ways, mp_ways = mesh.devices.shape
    fine_mesh = Mesh(
        mesh.devices.reshape(dp_ways // 2, 2, mp_ways // 2, 2), ("z", "y", "x", "c")
    )
    rows = P(("z", "y", "x", "c"), None)
    project = P(DP, None, MP)
    plain = P(DP, MP)
    slab_pair = P(DP, None, None, MP)
    slab_single = P(DP, None, MP)
    weights = (P(), P(), P(), project, plain, project, plain, slab_pair, slab_single)
    return jax.shard_map(
        local,
        mesh=fine_mesh,
        in_specs=(rows, rows, P(DP), P(DP), P(DP, None)) + weights + weights,
        out_specs=(rows, P(), rows) + weights + weights + weights,
        check_vma=False,
    )
```

```python
import functools

import jax
import jax.numpy as jnp
from jax import lax
from jax.experimental import pallas as pl
from jax.experimental.pallas import tpu as pltpu
from jax.sharding import Mesh
from jax.sharding import PartitionSpec as P

D = 768
HEADS = 12
HEAD_DIM = 64
FF = 2048

highest = lax.Precision.HIGHEST
bf16 = jnp.bfloat16
f32 = jnp.float32
norm_eps = 1e-06
rope_base = 10000.0
masked_score = -1e30
ns_first = 3.4445
ns_second = -4.775
ns_third = 2.0315
decay_rate = 0.5
gain_rate = 0.05
router_rate = 0.02

DP = ("z", "y")
MP = ("x", "c")
SPARE = 64
SWAP = ((0, 1), (1, 0))
BLOCK = 256
VMEM_BYTES = 56 * 1024 * 1024


def rms_scale(values):
    return lax.rsqrt(jnp.mean(values * values, axis=-1, keepdims=True) + norm_eps)


def rotate(values, cosine, sine_part):
    half_dim = values.shape[-1] // 2
    first_half = values[..., :half_dim]
    second = values[..., half_dim:]
    return jnp.concatenate(
        [first_half * cosine - second * sine_part, second * cosine + first_half * sine_part],
        axis=-1,
    )


def swiglu_back(gate_values, up_values, grad_inner):
    sigmoid_gate = jax.nn.sigmoid(gate_values)
    grad_gate_part = (
        grad_inner * up_values * sigmoid_gate * (1.0 + gate_values * (1.0 - sigmoid_gate))
    )
    grad_up_part = grad_inner * gate_values * sigmoid_gate
    return grad_gate_part.astype(bf16), grad_up_part.astype(bf16)


def norm_back(grad_normed, inputs, row_scale, norm_gain):
    scaled = grad_normed * norm_gain
    return row_scale * scaled - inputs * row_scale**3 * jnp.mean(
        scaled * inputs, axis=-1, keepdims=True
    )


def mm(left, right):
    return jnp.dot(left, right, preferred_element_type=f32)


def mm_t(left, right):
    return lax.dot_general(left, right, (((1,), (1,)), ((), ())), preferred_element_type=f32)


def t_mm(left, right):
    return lax.dot_general(left, right, (((0,), (0,)), ((), ())), preferred_element_type=f32)


def two_parts(values):
    high = lax.reduce_precision(values, exponent_bits=8, mantissa_bits=7)
    return high.astype(bf16), (values - high).astype(bf16)


def swap_cores(values):
    return lax.ppermute(values, "c", SWAP)


def swap_chips(values):
    return lax.ppermute(values, "x", SWAP)


def swap_groups(values, distance):
    size = lax.axis_size(DP)
    return lax.ppermute(values, DP, [(place, place ^ distance) for place in range(size)])


def few_groups():
    return lax.axis_size(DP) <= 8


def local_order(values, row_count):
    place = lax.axis_index(MP)
    blocks = [
        lax.dynamic_slice_in_dim(values, (place ^ flip) * row_count, row_count, 0)
        for flip in (0, 2, 1, 3)
    ]
    return jnp.concatenate(blocks, axis=0)


def turn_pair(values):
    half = values.shape[0] // 2
    return jnp.concatenate([values[half:], values[:half]], axis=0)


def reduce_rows(partial):
    half = partial.shape[0] // 2
    got = swap_cores(partial[half:].astype(bf16))
    mine = (partial[:half] + got.astype(f32)).astype(bf16)
    return mine.astype(f32) + turn_pair(swap_chips(mine)).astype(f32)


def join_rows(rows):
    return jnp.concatenate([rows, swap_cores(rows)], axis=0)


def gather_shards(values):
    if not few_groups():
        return lax.all_gather(values, DP, axis=0, tiled=True)
    size = lax.axis_size(DP)
    place = lax.axis_index(DP)
    rows = values.shape[0]
    full = jnp.zeros((size * rows, values.shape[1]), values.dtype)
    full = lax.dynamic_update_slice_in_dim(full, values, place * rows, 0)
    for distance in range(1, size):
        got = swap_groups(values, distance)
        full = lax.dynamic_update_slice_in_dim(full, got, (place ^ distance) * rows, 0)
    return full


def scatter_shards(values):
    parts = lax.all_to_all(values.astype(bf16), DP, split_axis=0, concat_axis=0, tiled=True)
    return jnp.sum(parts.reshape(lax.axis_size(DP), -1, values.shape[1]).astype(f32), axis=0)


def exchange(values):
    return lax.all_to_all(values, DP, split_axis=0, concat_axis=0, tiled=True)


def paired_view(values):
    count, width, _, units = values.shape
    tiles = units // 128
    return (
        values.reshape(count, width, 2, tiles, 128)
        .transpose(0, 1, 3, 2, 4)
        .reshape(count, width * 2 * tiles, 128)
    )


def split_kernel(values_ref, out_ref, *, tiles, rows):
    for place in range(2 * tiles):
        column = (place % 2) * tiles * 128 + (place // 2) * 128
        out_ref[:, column : column + 128] = values_ref[
            pl.ds(place, rows, stride=2 * tiles), :
        ].astype(bf16)


def split_pairs(values):
    count, width, _, units = values.shape
    tiles = units // 128
    rows = BLOCK
    return pl.pallas_call(
        functools.partial(split_kernel, tiles=tiles, rows=rows),
        grid=(count, width // rows),
        in_specs=[pl.BlockSpec((None, rows * 2 * tiles, 128), lambda i, j: (i, j, 0))],
        out_specs=pl.BlockSpec((None, rows, 2 * units), lambda i, j: (i, j, 0)),
        out_shape=jax.ShapeDtypeStruct((count, width, 2 * units), bf16),
        name="split_pairs",
    )(paired_view(values))


def gram_term(matrix):
    width = matrix.shape[0]
    return jnp.concatenate(
        [
            mm_t(matrix[start : start + BLOCK], matrix[start:]).astype(bf16)
            for start in range(0, width, BLOCK)
        ],
        axis=1,
    )


def step_kernel(mine_ref, other_ref, step_ref, inverse_ref, gram):
    width = gram.shape[0]
    total = mine_ref[0].astype(f32) + other_ref[0].astype(f32)
    row = lax.broadcasted_iota(jnp.int32, (BLOCK, BLOCK), 0)
    column = lax.broadcasted_iota(jnp.int32, (BLOCK, BLOCK), 1)
    place = 0
    trace = jnp.zeros((1, 1), f32)
    for start in range(0, width, BLOCK):
        for across in range(start, width, BLOCK):
            block = total[:, place : place + BLOCK]
            place += BLOCK
            gram[start : start + BLOCK, across : across + BLOCK] = block
            if across > start:
                gram[across : across + BLOCK, start : start + BLOCK] = block.T
            else:
                diagonal = jnp.where(row == column, block, 0.0)
                trace += jnp.sum(jnp.sum(diagonal, axis=1, keepdims=True), axis=0, keepdims=True)
    inverse = 1.0 / (trace + 1e-12)
    first_gram = gram[...] * inverse
    first_low = first_gram.astype(bf16)
    first_poly = (ns_second * first_gram + ns_third * mm(first_low, first_low)).astype(bf16)
    mixed = mm(first_poly, first_low)
    second_gram = (
        ns_first * ns_first * first_gram
        + 2.0 * ns_first * mixed
        + mm(mixed.astype(bf16), first_poly)
    )
    second_low = second_gram.astype(bf16)
    second_poly = (ns_second * second_gram + ns_third * mm(second_low, second_low)).astype(bf16)
    combined = ns_first * (first_poly.astype(f32) + second_poly.astype(f32)) + mm(
        second_poly, first_poly
    )
    step_ref[0] = combined.astype(bf16)
    inverse_ref[0] = jnp.broadcast_to(inverse, (8, 128))


def step_matrices(mine, other):
    count, _, packed = mine.shape
    width = 768
    spec = pl.BlockSpec((1, BLOCK, packed), lambda i: (i, 0, 0))
    steps, inverse = pl.pallas_call(
        step_kernel,
        grid=(count,),
        in_specs=[spec, spec],
        out_specs=[
            pl.BlockSpec((1, width, width), lambda i: (i, 0, 0)),
            pl.BlockSpec((1, 8, 128), lambda i: (i, 0, 0)),
        ],
        out_shape=[
            jax.ShapeDtypeStruct((count, width, width), bf16),
            jax.ShapeDtypeStruct((count, 8, 128), f32),
        ],
        scratch_shapes=[pltpu.VMEM((width, width), f32)],
        compiler_params=pltpu.CompilerParams(vmem_limit_bytes=VMEM_BYTES),
        name="step_matrices",
    )(mine, other)
    return steps, inverse


def solve_steps(matrices):
    first_core = lax.axis_index("c") == 0
    half = len(matrices) // 2
    grams = [gram_term(matrix) for matrix in matrices]
    early, late = jnp.stack(grams[:half]), jnp.stack(grams[half:])
    got = swap_cores(jnp.where(first_core, late, early))
    mine = (jnp.where(first_core, early, late).astype(f32) + got.astype(f32)).astype(bf16)
    steps, inverse = step_matrices(mine, swap_chips(mine))
    other_steps, other_inverse = swap_cores(steps), swap_cores(inverse)
    early_steps = jnp.where(first_core, steps, other_steps)
    late_steps = jnp.where(first_core, other_steps, steps)
    early_inverse = jnp.where(first_core, inverse, other_inverse)
    late_inverse = jnp.where(first_core, other_inverse, inverse)
    return [
        (pair[0][index], pair[1][index, 0, 0])
        for pair in ((early_steps, early_inverse), (late_steps, late_inverse))
        for index in range(half)
    ]


def normed_delta(moment, step_rate):
    return -step_rate * moment * lax.rsqrt(jnp.mean(moment * moment) + 1e-12)


def local(
    tokens,
    teacher,
    segments,
    valid_mask,
    routes,
    first_gain,
    second_gain,
    router_weight,
    attention_in,
    attention_out,
    dense_in,
    dense_out,
    expert_in,
    expert_out,
    moment_first_gain,
    moment_second_gain,
    moment_router,
    moment_attention_in,
    moment_attention_out,
    moment_dense_in,
    moment_dense_out,
    moment_expert_in,
    moment_expert_out,
):
    row_count, width = tokens.shape
    mp_ways = lax.axis_size(MP)
    dp_ways = lax.axis_size(DP)
    dp_place = lax.axis_index(DP)
    chip_place = lax.axis_index("x")
    core_place = lax.axis_index("c")
    first_core = core_place == 0
    seq_len = row_count * mp_ways
    expert_total = router_weight.shape[1]
    capacity = 4 * seq_len // expert_total
    half_cap = capacity // 2
    shard_rows = attention_in.shape[0]
    slabs = expert_in.shape[0]
    units = expert_in.shape[3]
    dense_units = dense_in.shape[2]
    sharing = FF // (units * mp_ways)
    heads_here = attention_in.shape[2] // HEAD_DIM
    head_cols = attention_in.shape[2]
    project_cols = 3 * head_cols
    project_scale = (3 * HEADS * HEAD_DIM / D) ** 0.5
    mix_scale = (HEADS * HEAD_DIM / D) ** 0.5
    pair_scale = (2 * FF / D) ** 0.5
    single_scale = (FF / D) ** 0.5
    slab_pair_scale = (2 * FF / (sharing * D)) ** 0.5
    slab_single_scale = (FF / (sharing * D)) ** 0.5
    by_slab = few_groups() and slabs % 2 == 0 and sharing == 1
    group = slabs // 2 if by_slab else slabs

    mask_float = valid_mask.astype(f32)
    own_count = jnp.sum(mask_float)
    high_count = jnp.floor(own_count / 256.0)
    count_cells = jnp.zeros((shard_rows, SPARE), f32)
    count_cells = count_cells.at[0, 0].set(high_count)
    count_cells = count_cells.at[1, 0].set(own_count - 256.0 * high_count)
    first_pack = jnp.concatenate(
        [attention_in.reshape(shard_rows, project_cols), count_cells, attention_out], axis=1
    ).astype(bf16)
    first_full = gather_shards(first_pack)
    weight_project = first_full[:, :project_cols]
    weight_mix = first_full[:, project_cols + SPARE :]
    counts = first_full[:, project_cols].astype(f32).reshape(dp_ways, shard_rows)
    valid_count = jnp.sum(256.0 * counts[:, 0] + counts[:, 1])
    tokens_pair = jnp.concatenate([tokens, swap_chips(tokens)], axis=0)
    teacher_pair = jnp.concatenate([teacher, swap_chips(teacher)], axis=0)
    second_pack = jnp.concatenate(
        [dense_in[:, 0, :], dense_in[:, 1, :], dense_out], axis=1
    ).astype(bf16)
    second_full = gather_shards(second_pack)
    weight_pair = second_full[:, : 2 * dense_units]
    weight_down = second_full[:, 2 * dense_units :]
    router_low = router_weight.astype(bf16)
    expert_pair = split_pairs(expert_in)
    expert_down = expert_out.astype(bf16)
    if by_slab:
        kept = lax.dynamic_slice_in_dim(expert_pair, core_place * group, group, 0)
        sent = lax.dynamic_slice_in_dim(expert_pair, (1 - core_place) * group, group, 0)
        got = swap_cores(sent)
        expert_gate = jnp.concatenate([kept[:, :, :units], got[:, :, :units]], axis=2)
        expert_up = jnp.concatenate([kept[:, :, units:], got[:, :, units:]], axis=2)
        kept = lax.dynamic_slice_in_dim(expert_down, core_place * group, group, 0)
        sent = lax.dynamic_slice_in_dim(expert_down, (1 - core_place) * group, group, 0)
        expert_down = jnp.concatenate([kept, swap_cores(sent)], axis=2)
    else:
        expert_gate = expert_pair[:, :, :units]
        expert_up = expert_pair[:, :, units:]

    order = local_order(jnp.arange(seq_len, dtype=jnp.int32), row_count)
    names = local_order(routes, row_count)
    documents = local_order(segments, row_count)
    onehot = (
        names[:, :, None] == jnp.arange(expert_total, dtype=jnp.int32)[None, None, :]
    ).astype(f32)
    earlier = mm(
        (order[:, None] > order[None, :]).astype(bf16), jnp.sum(onehot, axis=1).astype(bf16)
    )
    ranks = jnp.sum(onehot * earlier[:, None, :], axis=-1).astype(jnp.int32)
    if by_slab:
        half_ranks = ranks - chip_place * half_cap
        lanes = names % slabs
        here = lanes // group == core_place
        slot_rows = ((names // slabs) ^ dp_place) * group + lanes % group
        slot_total = dp_ways * group * half_cap
    else:
        half_ranks = ranks - core_place * half_cap
        here = True
        slot_rows = names
        slot_total = expert_total * half_cap
    here = here & (half_ranks >= 0) & (half_ranks < half_cap)
    slot_ids = jnp.where(here, slot_rows * half_cap + half_ranks, -1)
    slot_order = jnp.arange(slot_total, dtype=jnp.int32)
    picks = [(slot_ids[:, k][:, None] == slot_order[None, :]) for k in range(2)]
    select = (picks[0] | picks[1]).astype(bf16)

    def to_owners(rows):
        if by_slab:
            chunks = rows.reshape(dp_ways, group * half_cap, width)
            mine, other = [chunks[0]], []
            for distance in range(1, dp_ways):
                mine.append(swap_groups(chunks[distance], distance))
            for chunk in mine:
                other.append(swap_chips(chunk))
            whole = jnp.stack(mine + other).reshape(2 * dp_ways, group, half_cap, width)
            return [whole[:, slab].reshape(-1, width) for slab in range(group)]
        spread = jnp.broadcast_to(
            rows.reshape(expert_total, 1, half_cap, width),
            (expert_total, sharing, half_cap, width),
        ).reshape(expert_total * sharing, half_cap, width)
        moved = exchange(spread).reshape(dp_ways, slabs, half_cap, width)
        both = lax.all_gather(moved, "c", axis=0)
        return [both[:, :, slab].reshape(-1, width) for slab in range(slabs)]

    def to_sources(parts):
        if by_slab:
            whole = jnp.stack(
                [part.reshape(2, dp_ways, half_cap, width) for part in parts], axis=2
            )
            step = 2 if dp_ways > 2 else 1
            back = []
            for start in range(0, dp_ways, step):
                got = swap_chips(whole[1, start : start + step].astype(bf16))
                total = (whole[0, start : start + step].astype(f32) + got.astype(f32)).astype(bf16)
                for distance in range(start, start + step):
                    chunk = total[distance - start]
                    back.append(swap_groups(chunk, distance) if distance else chunk)
            return jnp.stack(back).reshape(slot_total, width)
        stacked = jnp.stack(
            [part.reshape(2, dp_ways, half_cap, width) for part in parts], axis=2
        ).astype(bf16)
        swapped = lax.all_to_all(stacked, "c", split_axis=0, concat_axis=0, tiled=True)
        halves = (swapped[0].astype(f32) + swapped[1].astype(f32)).astype(bf16)
        moved = exchange(halves.reshape(dp_ways * slabs, half_cap, width))
        moved = moved.reshape(expert_total, sharing, half_cap, width)
        if sharing > 1:
            moved = jnp.sum(moved.astype(f32), axis=1).astype(bf16)
        return moved.reshape(slot_total, width)

    token_float = tokens_pair.astype(f32)
    scale_one = rms_scale(token_float)
    full_one = join_rows((token_float * scale_one * first_gain).astype(bf16))
    projected = mm(full_one, weight_project).reshape(seq_len, 3, heads_here, HEAD_DIM)
    frequency = rope_base ** (-jnp.arange(HEAD_DIM // 2, dtype=f32) * 2.0 / HEAD_DIM)
    angles = order.astype(f32)[:, None] * frequency[None, :]
    cosine = jnp.cos(angles)[:, None, :]
    sine = jnp.sin(angles)[:, None, :]
    query_scale = HEAD_DIM ** (-0.5)
    queries = (rotate(projected[:, 0], cosine, sine) * query_scale).astype(bf16)
    key_rows = rotate(projected[:, 1], cosine, sine).astype(bf16)
    value_rows = projected[:, 2].astype(bf16)
    allowed = (documents[:, None] == documents[None, :]) & (order[:, None] >= order[None, :])

    def head_scores():
        scores = jnp.einsum("qhd,khd->hqk", queries, key_rows, preferred_element_type=f32)
        return jnp.where(allowed[None], scores, masked_score)

    scores = head_scores()
    row_peak = jnp.max(scores, axis=-1, keepdims=True)
    exponent = jnp.exp(scores - row_peak)
    row_total = jnp.sum(exponent, axis=-1, keepdims=True)
    probs = exponent / row_total
    probs_low = probs.astype(bf16)
    mixed_low = (
        jnp.einsum("hqk,khd->qhd", probs_low, value_rows, preferred_element_type=f32)
        .astype(bf16)
        .reshape(seq_len, head_cols)
    )
    log_totals = row_peak + jnp.log(row_total)
    hidden = token_float + reduce_rows(mm_t(mixed_low, weight_mix))
    scale_two = rms_scale(hidden)
    full_two = join_rows((hidden * scale_two * second_gain).astype(bf16))

    received = to_owners(t_mm(select, full_two).astype(bf16))

    gate_up = mm(full_two, weight_pair)
    gate_part = gate_up[:, :dense_units]
    up_part = gate_up[:, dense_units:]
    dense_inner = (jax.nn.silu(gate_part) * up_part).astype(bf16)
    dense_part = mm_t(dense_inner, weight_down)
    logits = mm(full_two, router_low)
    chosen = jnp.sum(onehot * logits[:, None, :], axis=-1)
    gate_probs = jax.nn.softmax(chosen, axis=-1)
    weighted = (
        jnp.where(picks[0], gate_probs[:, 0:1], 0.0) + jnp.where(picks[1], gate_probs[:, 1:2], 0.0)
    ).astype(bf16)

    slab_gate, slab_up, slab_inner, slab_parts = [], [], [], []
    for slab in range(group):
        gate_values = mm(received[slab], expert_gate[slab])
        up_values = mm(received[slab], expert_up[slab])
        inner = (jax.nn.silu(gate_values) * up_values).astype(bf16)
        slab_gate.append(gate_values)
        slab_up.append(up_values)
        slab_inner.append(inner)
        slab_parts.append(mm_t(inner, expert_down[slab]).astype(bf16))
    expert_rows = to_sources(slab_parts)
    output = hidden + reduce_rows(dense_part + mm(weighted, expert_rows))
    errors = output - teacher_pair.astype(f32)
    pair_mask = local_order(mask_float, row_count)[: 2 * row_count]
    loss_local = jnp.sum(jnp.sum(errors * errors, axis=-1)[:row_count] * pair_mask[:row_count])
    factor = seq_len * dp_ways / valid_count
    grad_output = errors * (pair_mask * factor)[:, None]
    grad_branch = join_rows(grad_output.astype(bf16))

    raw_slots = t_mm(select, grad_branch)
    slot_gates = jnp.sum(
        jnp.where(picks[0], gate_probs[:, 0:1], 0.0) + jnp.where(picks[1], gate_probs[:, 1:2], 0.0),
        axis=0,
    )
    grad_received = to_owners((raw_slots * slot_gates[:, None]).astype(bf16))
    slot_dots = jnp.sum(raw_slots * expert_rows.astype(f32), axis=-1)
    grad_chosen_raw = jnp.stack(
        [jnp.sum(jnp.where(pick, slot_dots[None, :], 0.0), axis=-1) for pick in picks], axis=-1
    )
    grad_chosen = gate_probs * (
        grad_chosen_raw - jnp.sum(gate_probs * grad_chosen_raw, axis=-1, keepdims=True)
    )
    grad_logits = jnp.sum(onehot * grad_chosen[:, :, None], axis=1)
    logits_high, logits_rest = two_parts(grad_logits)
    grad_router = t_mm(full_two, logits_high) + t_mm(full_two, logits_rest)

    grad_dense_inner = mm(grad_branch, weight_down)
    grad_gate, grad_up = swiglu_back(gate_part, up_part, grad_dense_inner)
    grad_pair = jnp.concatenate([grad_gate, grad_up], axis=1)
    grad_down = t_mm(grad_branch, dense_inner)
    grad_dense_in = t_mm(full_two, grad_pair)
    grad_full_two = (
        mm_t(grad_pair, weight_pair) + mm_t(logits_high, router_low) + mm_t(logits_rest, router_low)
    )

    slab_dispatch, grad_in_slabs, grad_out_slabs = [], [], []
    for slab in range(group):
        grad_inner = mm(grad_received[slab], expert_down[slab])
        grad_g, grad_u = swiglu_back(slab_gate[slab], slab_up[slab], grad_inner)
        slab_dispatch.append(
            (mm_t(grad_g, expert_gate[slab]) + mm_t(grad_u, expert_up[slab])).astype(bf16)
        )
        grad_in_slabs.append((t_mm(received[slab], grad_g), t_mm(received[slab], grad_u)))
        grad_out_slabs.append(t_mm(grad_received[slab], slab_inner[slab]))
    grad_slot_rows = to_sources(slab_dispatch)
    grad_normed_two = reduce_rows(grad_full_two + mm(select, grad_slot_rows))
    dense_shard = scatter_shards(jnp.concatenate([grad_dense_in, grad_down], axis=1))

    if by_slab:
        stacked = jnp.stack(
            [
                jnp.concatenate([gate_grad, up_grad, down_grad], axis=1)
                for (gate_grad, up_grad), down_grad in zip(grad_in_slabs, grad_out_slabs)
            ]
        ).reshape(group, width, 3, 2, units)
        kept = stacked[:, :, :, 0]
        got = swap_cores(stacked[:, :, :, 1].astype(bf16)).astype(f32)
        both = jnp.concatenate(
            [jnp.where(first_core, kept, got), jnp.where(first_core, got, kept)], axis=0
        )
        grad_expert_in = both[:, :, :2]
        grad_expert_out = both[:, :, 2]
    else:
        grad_expert_in = jnp.stack([jnp.stack(pair, axis=1) for pair in grad_in_slabs])
        grad_expert_out = jnp.stack(grad_out_slabs)
    new_moment_expert_in = decay_rate * moment_expert_in + grad_expert_in
    new_moment_expert_out = decay_rate * moment_expert_out + grad_expert_out
    expert_matrices = []
    for slab in range(slabs):
        expert_matrices.append(
            jnp.concatenate(
                [new_moment_expert_in[slab, :, 0, :], new_moment_expert_in[slab, :, 1, :]], axis=1
            ).astype(bf16)
        )
        expert_matrices.append(new_moment_expert_out[slab].astype(bf16))
    expert_steps = solve_steps(expert_matrices)
    shard_pair = dense_shard[:, : 2 * dense_units].reshape(shard_rows, 2, dense_units)
    shard_down = dense_shard[:, 2 * dense_units :]
    new_moment_pair = decay_rate * moment_dense_in + shard_pair
    new_moment_down = decay_rate * moment_dense_out + shard_down
    dense_moments = lax.all_gather(
        jnp.concatenate(
            [new_moment_pair[:, 0, :], new_moment_pair[:, 1, :], new_moment_down], axis=1
        ).astype(bf16),
        DP,
        axis=0,
        tiled=True,
    )
    full_pair = dense_moments[:, : 2 * dense_units]
    full_down = dense_moments[:, 2 * dense_units :]
    dense_steps = solve_steps([full_pair, full_down])

    grad_hidden = norm_back(grad_normed_two, hidden, scale_two, second_gain) + grad_output
    grad_second_part = jnp.sum((grad_normed_two * hidden * scale_two)[:row_count], axis=0)
    grad_attended = join_rows(grad_hidden.astype(bf16))
    grad_mix = t_mm(grad_attended, mixed_low)
    grad_mixed = (
        mm(grad_attended, weight_mix).astype(bf16).reshape(seq_len, heads_here, HEAD_DIM)
    )
    score_weights = jnp.exp(head_scores() - log_totals)
    grad_weights = jnp.einsum("qhd,khd->hqk", grad_mixed, value_rows, preferred_element_type=f32)
    row_dots = jnp.sum(grad_weights * score_weights, axis=-1, keepdims=True)
    grad_scores = (score_weights * (grad_weights - row_dots)).astype(bf16)
    grad_queries = jnp.einsum("hqk,khd->qhd", grad_scores, key_rows, preferred_element_type=f32)
    grad_keys = jnp.einsum("hqk,qhd->khd", grad_scores, queries, preferred_element_type=f32)
    grad_values = jnp.einsum(
        "hqk,qhd->khd", score_weights.astype(bf16), grad_mixed, preferred_element_type=f32
    )
    grad_projected = jnp.concatenate(
        [
            rotate(grad_queries * query_scale, cosine, -sine).reshape(seq_len, head_cols),
            rotate(grad_keys, cosine, -sine).reshape(seq_len, head_cols),
            grad_values.reshape(seq_len, head_cols),
        ],
        axis=1,
    ).astype(bf16)
    grad_project = t_mm(full_one, grad_projected)
    grad_full_one = mm_t(grad_projected, weight_project)
    grad_first_part = jnp.sum(grad_full_one * full_one.astype(f32), axis=0) / first_gain

    loss_cells = jnp.zeros((width, 1), f32).at[0, 0].set(loss_local)
    small = jnp.concatenate(
        [grad_first_part[:, None], grad_second_part[:, None], grad_router, loss_cells], axis=1
    )
    small = jnp.pad(small, ((0, 0), (0, SPARE // 2 - small.shape[1])))
    small = jnp.concatenate(two_parts(small), axis=1)
    last_shard = scatter_shards(jnp.concatenate([grad_project.astype(bf16), small, grad_mix.astype(bf16)], axis=1))
    shard_project = last_shard[:, :project_cols].reshape(shard_rows, 3, head_cols)
    shard_mix = last_shard[:, project_cols + SPARE :]
    new_moment_project = decay_rate * moment_attention_in + shard_project
    new_moment_mix = decay_rate * moment_attention_out + shard_mix
    small = last_shard[:, project_cols : project_cols + SPARE // 2]
    small = small + last_shard[:, project_cols + SPARE // 2 : project_cols + SPARE]
    last_moments = gather_shards(
        jnp.concatenate(
            [
                new_moment_project.reshape(shard_rows, project_cols).astype(bf16),
                *two_parts(small),
                new_moment_mix.astype(bf16),
            ],
            axis=1,
        )
    )
    full_project = last_moments[:, :project_cols]
    full_mix = last_moments[:, project_cols + SPARE :]
    last_steps = solve_steps([full_project, full_mix])
    small_pair = last_moments[:, project_cols : project_cols + SPARE].astype(f32)
    small_part = small_pair[:, : SPARE // 2] + small_pair[:, SPARE // 2 :]
    small_part = small_part + swap_cores(small_part)
    small_total = small_part + swap_chips(small_part)
    grad_normed_one = reduce_rows(grad_full_one)
    grad_tokens = norm_back(grad_normed_one, token_float, scale_one, first_gain) + grad_hidden

    first_total = small_total[:, 0]
    second_total = small_total[:, 1]
    router_total = small_total[:, 2 : 2 + expert_total]
    loss_total = small_total[0, 2 + expert_total]
    loss_value = loss_total / (valid_count * width)
    new_moment_first = decay_rate * moment_first_gain + first_total
    new_moment_second = decay_rate * moment_second_gain + second_total
    new_moment_router = decay_rate * moment_router + router_total

    def update(solved, matrix, step_scale):
        step, inverse = solved
        full = ns_first * ns_first * matrix.astype(f32) + mm(step, matrix)
        return (-step_scale * jnp.sqrt(inverse)) * full

    def update_rows(solved, matrix, step_scale):
        step, inverse = solved
        step_rows = lax.dynamic_slice_in_dim(step, dp_place * shard_rows, shard_rows, 0)
        own_rows = lax.dynamic_slice_in_dim(matrix, dp_place * shard_rows, shard_rows, 0)
        full = ns_first * ns_first * own_rows.astype(f32) + mm(step_rows, matrix)
        return (-step_scale * jnp.sqrt(inverse)) * full

    step_first = normed_delta(new_moment_first, gain_rate)
    step_second = normed_delta(new_moment_second, gain_rate)
    new_router = router_weight + normed_delta(new_moment_router, router_rate)
    new_attention_in = attention_in + update_rows(
        last_steps[0], full_project, project_scale
    ).reshape(attention_in.shape)
    step_mix = update_rows(last_steps[1], full_mix, mix_scale)
    new_dense_in = dense_in + update_rows(dense_steps[0], full_pair, pair_scale).reshape(
        dense_in.shape
    )
    new_dense_out = dense_out + update_rows(dense_steps[1], full_down, single_scale)
    pair_steps, single_steps = [], []
    for slab in range(slabs):
        pair_steps.append(
            update(expert_steps[2 * slab], expert_matrices[2 * slab], slab_pair_scale).reshape(
                width, 2, units
            )
        )
        single_steps.append(
            update(expert_steps[2 * slab + 1], expert_matrices[2 * slab + 1], slab_single_scale)
        )
    new_expert_in = expert_in + jnp.stack(pair_steps)
    new_expert_out = expert_out + jnp.stack(single_steps)
    return (
        output[:row_count].astype(bf16),
        loss_value,
        grad_tokens[:row_count],
        first_total,
        second_total,
        router_total,
        shard_project,
        shard_mix,
        shard_pair,
        shard_down,
        grad_expert_in,
        grad_expert_out,
        new_moment_first,
        new_moment_second,
        new_moment_router,
        new_moment_project,
        new_moment_mix,
        new_moment_pair,
        new_moment_down,
        new_moment_expert_in,
        new_moment_expert_out,
        step_first,
        step_second,
        new_router,
        new_attention_in,
        step_mix,
        new_dense_in,
        new_dense_out,
        new_expert_in,
        new_expert_out,
    )


def solution(mesh):
    dp_ways, mp_ways = mesh.devices.shape
    fine_mesh = Mesh(
        mesh.devices.reshape(dp_ways // 2, 2, mp_ways // 2, 2), ("z", "y", "x", "c")
    )
    rows = P(("z", "y", "x", "c"), None)
    project = P(DP, None, MP)
    plain = P(DP, MP)
    slab_pair = P(DP, None, None, MP)
    slab_single = P(DP, None, MP)
    weights = (P(), P(), P(), project, plain, project, plain, slab_pair, slab_single)
    return jax.shard_map(
        local,
        mesh=fine_mesh,
        in_specs=(rows, rows, P(DP), P(DP), P(DP, None)) + weights + weights,
        out_specs=(rows, P(), rows) + weights + weights + weights,
        check_vma=False,
    )
```
